32 devices in a mesh: section: 2 (over y), dp: 4 (over x, core), shard: 4 (over z).
Axes of the slice: x: 2, y: 2, z: 4, core: 2. Of those that a mesh axis runs over, the one named last changes fastest.
Arguments:
- features: bfloat16 [2, 512, 6144], P('section', ('dp', 'shard')), may hold values from -6 to 6
- delayed_error: bfloat16 [2, 512, 6144], P('section', ('dp', 'shard')), may hold values from -6 to 6
- ln_gain: float32 [2, 6144], P('section'), may hold values from 0.25 to 1.75
- w_in: bfloat16 [2, 6144, 12288], P('section', None, 'shard'), may hold values from -0.078125 to 0.078125
- w_out: bfloat16 [2, 12288, 6144], P('section', 'shard'), may hold values from -0.0546875 to 0.0546875
Outputs:
- passed_error: bfloat16 [2, 512, 6144], P('section', ('dp', 'shard'))
- gain_grad: float32 [2, 6144], P('section')
- w_in_grad: bfloat16 [2, 6144, 12288], P('section', 'dp', 'shard')
- w_out_grad: bfloat16 [2, 12288, 6144], P('section', 'shard', 'dp')
The draws below stay inside these ranges and needn't reach their ends.
All inputs are finite; a program needn't handle non-finite values.
Results may differ from the reference program's by a relative error of at most 0.013.
Values may be sent and summed in bfloat16 or wider, within the bound.
No kernel may reach another device: no remote copies, remote signals or barrier semaphores. Data moves between devices by JAX's collectives and lax.ppermute only.
A program may use at most 256 MiB of HBM per device.

```python
import jax
import jax.numpy as jnp
from jax import lax

D = 6144
FF = 12288
TOK_DEV = 32
TOKENS = 512
SECTIONS = 2
N_SECTION = 2
N_DP = 4
N_SHARD = 4


def shard_levels(key, extent, split, smallest, top_value):
    def one(dim, blocks):
        steps = jax.random.uniform(jax.random.fold_in(jax.random.fold_in(key, 6), dim), (blocks,), jnp.float32, smallest / len(split), top_value / len(split))
        return jnp.repeat(jnp.exp(steps), extent[dim] // blocks).reshape((-1,) + (1,) * (len(extent) - dim - 1))

    loudness = one(*split[0])
    for cut in split[1:]:
        loudness = loudness * one(*cut)
    return loudness


def scatter_about(own_key, shape, deviation, limit, pieces=(), kind=jnp.bfloat16):
    array = jax.random.normal(own_key, shape, jnp.float32) * deviation
    if len(pieces) > 0:
        array = shard_levels(own_key, shape, pieces, -0.22, 0.18) * array
    return jnp.clip(array, min=-limit, max=limit).astype(kind)


def setup_inputs(seed: int = 0) -> dict:
    keys = jax.random.split(jax.random.key(seed), 6)
    features = scatter_about(keys[0], (SECTIONS, TOKENS, D), 1.0, 6.0, ((0, 2), (1, 16)))
    delayed_error = scatter_about(keys[1], (SECTIONS, TOKENS, D), 1.0, 6.0, ((0, 2), (1, 16)))
    ln_gain = jnp.clip(1.0 + 0.15 * jax.random.normal(keys[2], (SECTIONS, D), jnp.float32), 0.25, 1.75)
    w_in = scatter_about(keys[3], (SECTIONS, D, FF), D ** -0.5, 0.078125, ((0, 2), (2, 4)))
    w_out = scatter_about(keys[4], (SECTIONS, FF, D), FF ** -0.5, 0.0546875, ((0, 2), (1, 4)))
    return dict(features=features, delayed_error=delayed_error, ln_gain=ln_gain, w_in=w_in, w_out=w_out)


SQRT_HALF = 0.7071067811865476
INV_ROOT_TWO_PI = 0.3989422804014327
EPSILON = 1e-06

def rounded(values):
    return lax.optimization_barrier(values.astype(jnp.bfloat16)).astype(jnp.float32)

def one_module(features, errors, scale, w_in, w_out):
    values = features.astype(jnp.float32)
    average = lax.optimization_barrier(jnp.mean(values, -1, keepdims=True))
    centred = values - average
    variance = lax.optimization_barrier(jnp.mean(centred * centred, -1, keepdims=True))
    inverse = lax.rsqrt(variance + EPSILON)
    centred = centred * inverse
    normed = (centred * scale).astype(jnp.bfloat16)
    pre = jnp.dot(normed, w_in, preferred_element_type=jnp.float32)
    normal_cdf = 0.5 * (1.0 + jax.scipy.special.erf(pre * SQRT_HALF))
    density = INV_ROOT_TWO_PI * jnp.exp(-0.5 * pre * pre)
    active = (pre * normal_cdf).astype(jnp.bfloat16)
    back_act = jnp.dot(errors, w_out.T, preferred_element_type=jnp.float32)
    pre_error = (back_act * (normal_cdf + pre * density)).astype(jnp.bfloat16)
    width = FF // N_SHARD
    norm_error = jnp.zeros((TOKENS, D), jnp.float32)
    for column_block in range(N_SHARD):
        lower = column_block * width
        term = jnp.dot(pre_error[:, lower:lower + width], w_in[:, lower:lower + width].T, preferred_element_type=jnp.float32)
        norm_error = norm_error + rounded(term)
    scaled = norm_error * scale
    corrected = inverse * (scaled - lax.optimization_barrier(jnp.mean(scaled, -1, keepdims=True)) - centred * lax.optimization_barrier(jnp.mean(scaled * centred, -1, keepdims=True)))
    own_error = (errors.astype(jnp.float32) + corrected).astype(jnp.bfloat16)
    gain_grad = lax.optimization_barrier(jnp.sum(norm_error * centred, 0))
    group = TOK_DEV * N_SHARD
    in_grad = jnp.zeros((D, FF), jnp.float32)
    out_grad = jnp.zeros((FF, D), jnp.float32)
    for group_index in range(N_DP):
        lower = group_index * group
        in_grad = in_grad + rounded(jnp.dot(normed[lower:lower + group].T, pre_error[lower:lower + group], preferred_element_type=jnp.float32))
        out_grad = out_grad + rounded(jnp.dot(active[lower:lower + group].T, errors[lower:lower + group], preferred_element_type=jnp.float32))
    return (own_error, gain_grad, in_grad.astype(jnp.bfloat16), out_grad.astype(jnp.bfloat16))

def reference(features, delayed_error, ln_gain, w_in, w_out):
    results = []
    for section_number in range(N_SECTION):
        results.append(one_module(features[section_number], delayed_error[section_number], ln_gain[section_number], w_in[section_number], w_out[section_number]))
    passed_error = jnp.stack([results[(section_number + 1) % N_SECTION][0] for section_number in range(N_SECTION)])
    gain_grad = jnp.stack([entry[1] for entry in results])
    w_in_grad = jnp.stack([entry[2] for entry in results])
    w_out_grad = jnp.stack([entry[3] for entry in results])
    return (passed_error, gain_grad, w_in_grad, w_out_grad)
```

```python
import functools

import jax
import jax.numpy as jnp
from jax import lax
from jax.experimental import pallas as pl
from jax.experimental.pallas import tpu as pltpu
from jax.sharding import PartitionSpec as P

SQRT_HALF = 0.7071067811865476
INV_ROOT_TWO_PI = 0.3989422804014327
EPSILON = 1e-06
VMEM_BYTES = 40 * 1024 * 1024


def tile_of(extent, largest=512):
    for size in (512, 384, 256, 128):
        if size <= largest and extent % size == 0:
            return size
    return extent


def params(grid=1):
    return pltpu.CompilerParams(
        vmem_limit_bytes=VMEM_BYTES, dimension_semantics=("arbitrary",) * grid
    )


def cost(flops, moved):
    return pl.CostEstimate(flops=int(flops), bytes_accessed=int(moved), transcendentals=0)


def dot(a, b, a_dim, b_dim):
    return lax.dot_general(
        a, b, (((a_dim,), (b_dim,)), ((), ())), preferred_element_type=jnp.float32
    )


def whole(shape):
    return pl.BlockSpec(shape, lambda *_: (0,) * len(shape))


def norm_kernel(hi_ref, x_ref, e_ref, g_ref, n_far, n_near, e_far, e_near, full):
    half = n_far.shape[1]
    values = x_ref[...].astype(jnp.float32)
    centred = values - jnp.mean(values, -1, keepdims=True)
    variance = jnp.mean(centred * centred, -1, keepdims=True)
    full[...] = centred * lax.rsqrt(variance + EPSILON) * g_ref[...]
    near = pl.ds(pl.multiple_of(hi_ref[0] * half, half), half)
    far = pl.ds(pl.multiple_of((1 - hi_ref[0]) * half, half), half)
    n_far[...] = full[:, far].astype(n_far.dtype)
    n_near[...] = full[:, near].astype(n_near.dtype)
    e_far[...] = e_ref[:, far]
    e_near[...] = e_ref[:, near]


def norm_halves(hi, x, e, gain):
    rows, width = x.shape
    half = jax.ShapeDtypeStruct((rows, width // 2), x.dtype)
    return pl.pallas_call(
        norm_kernel,
        out_shape=[half] * 4,
        grid_spec=pltpu.PrefetchScalarGridSpec(
            num_scalar_prefetch=1,
            grid=(1,),
            in_specs=[whole(x.shape), whole(e.shape), whole(gain.shape)],
            out_specs=[whole(half.shape)] * 4,
            scratch_shapes=[pltpu.VMEM(x.shape, jnp.float32)],
        ),
        compiler_params=params(),
        cost_estimate=cost(10 * x.size, 8 * x.size),
    )(hi, x, e, gain)


def part_kernel(count, dim, stage, _, *refs):
    blocks, refs = refs[:count], refs[count:]
    w_ref, refs = refs[0], refs[1:]
    group = refs[-1]

    @pl.when(pl.program_id(0) == 0)
    def _():
        rows = blocks[0].shape[0]
        for k, block in enumerate(blocks):
            group[k * rows:(k + 1) * rows, :] = block[...]

    total = dot(group[...], w_ref[...], 1, dim)
    if stage == "first":
        refs[0][...] = total
    elif stage == "active":
        prior, active, slope = refs[:3]
        pre = prior[...] + total
        normal_cdf = 0.5 * (1.0 + lax.erf(pre * SQRT_HALF))
        density = INV_ROOT_TWO_PI * jnp.exp(-0.5 * pre * pre)
        active[...] = (pre * normal_cdf).astype(active.dtype)
        slope[...] = normal_cdf + pre * density
    else:
        prior, slope, pre_error = refs[:3]
        pre_error[...] = ((prior[...] + total) * slope[...]).astype(pre_error.dtype)


def part(which, blocks, weight, dim, stage, extra=()):
    rows, half = blocks[0].shape
    tokens = rows * len(blocks)
    hidden = weight.shape[1 - dim]
    tile = tile_of(hidden)
    kind = blocks[0].dtype
    if dim == 0:
        w_spec = pl.BlockSpec((half, tile), lambda j, s: (s[0], j))
    else:
        w_spec = pl.BlockSpec((tile, half), lambda j, s: (j, s[0]))
    column = pl.BlockSpec((tokens, tile), lambda j, s: (0, j))
    wide = jax.ShapeDtypeStruct((tokens, hidden), jnp.float32)
    narrow = jax.ShapeDtypeStruct((tokens, hidden), kind)
    outs = {"first": [wide], "active": [narrow, wide], "error": [narrow]}[stage]
    return pl.pallas_call(
        functools.partial(part_kernel, len(blocks), dim, stage),
        out_shape=outs + [jax.ShapeDtypeStruct((tokens, half), kind)],
        grid_spec=pltpu.PrefetchScalarGridSpec(
            num_scalar_prefetch=1,
            grid=(hidden // tile,),
            in_specs=[whole((rows, half))] * len(blocks) + [w_spec] + [column] * len(extra),
            out_specs=[column] * len(outs) + [whole((tokens, half))],
        ),
        compiler_params=params(),
        cost_estimate=cost(2 * tokens * half * hidden, 2 * half * hidden),
    )(which, *blocks, weight, *extra)


def back_kernel(count, _, p_ref, w_ref, n_ref, g_ref, *outs):
    rows = outs[0].shape[0]
    term = dot(p_ref[...], w_ref[...], 1, 1).astype(outs[0].dtype)
    for k in range(count):
        outs[k][...] = term[k * rows:(k + 1) * rows, :]
    product = term.astype(jnp.float32) * n_ref[...].astype(jnp.float32)
    outs[count][...] = jnp.sum(product, 0, keepdims=True) / g_ref[...]


def back(which, count, pre_error, w_in, normed, gain):
    tokens, hidden = pre_error.shape
    half = normed.shape[1]
    tile = tile_of(half)
    steps = half // tile
    column = lambda j, s: (0, j)
    return pl.pallas_call(
        functools.partial(back_kernel, count),
        out_shape=[jax.ShapeDtypeStruct((tokens // count, half), normed.dtype)] * count
        + [jax.ShapeDtypeStruct((1, half), jnp.float32)],
        grid_spec=pltpu.PrefetchScalarGridSpec(
            num_scalar_prefetch=1,
            grid=(steps,),
            in_specs=[
                whole(pre_error.shape),
                pl.BlockSpec((tile, hidden), lambda j, s: (s[0] * steps + j, 0)),
                pl.BlockSpec((tokens, tile), column),
                pl.BlockSpec((1, tile), lambda j, s: (0, s[0] * steps + j)),
            ],
            out_specs=[pl.BlockSpec((tokens // count, tile), column)] * count
            + [pl.BlockSpec((1, tile), column)],
        ),
        compiler_params=params(),
        cost_estimate=cost(2 * tokens * half * hidden, 2 * half * hidden),
    )(which, pre_error, w_in, normed, gain)


def grad_kernel(count, cut_rows, _, *refs):
    cut, full, (out, a_all, b_all) = refs[:count], refs[count:2 * count], refs[2 * count:]
    rows = cut[0].shape[0]

    @pl.when(pl.program_id(0) == 0)
    def _():
        for k in range(count):
            a_all[k * rows:(k + 1) * rows, :] = cut[k][...]
            b_all[k * rows:(k + 1) * rows, :] = full[k][...]

    size = out.shape[0]
    window = pl.ds(pl.multiple_of(pl.program_id(0) * size, size), size)
    if cut_rows:
        out[...] = dot(a_all[:, window], b_all[...], 0, 0).astype(out.dtype)
    else:
        out[...] = dot(b_all[:, window], a_all[...], 0, 0).astype(out.dtype)


def grad(lo, cut, full, cut_rows):
    rows, hidden = full[0].shape
    width = cut[0].shape[1] // 2
    count = len(full)
    shape = (width, hidden) if cut_rows else (hidden, width)
    tile = tile_of(shape[0], 256 if cut_rows else 512)
    return pl.pallas_call(
        functools.partial(grad_kernel, count, cut_rows),
        out_shape=jax.ShapeDtypeStruct(shape, full[0].dtype),
        grid_spec=pltpu.PrefetchScalarGridSpec(
            num_scalar_prefetch=1,
            grid=(shape[0] // tile,),
            in_specs=[pl.BlockSpec((rows, width), lambda j, s: (0, s[0]))] * count
            + [whole((rows, hidden))] * count,
            out_specs=pl.BlockSpec((tile, shape[1]), lambda j, s: (j, 0)),
            scratch_shapes=[
                pltpu.VMEM((count * rows, width), full[0].dtype),
                pltpu.VMEM((count * rows, hidden), full[0].dtype),
            ],
        ),
        compiler_params=params(),
        cost_estimate=cost(2 * count * rows * width * hidden, 2 * width * hidden),
    )(lo, *cut, *full)


def own_kernel(count, flag_ref, x_ref, e_ref, g_ref, *refs):
    out, scaled_ref = refs[2 * count:]
    half = refs[0].shape[1]
    hi, last = flag_ref[0], flag_ref[1]
    for k, place in enumerate((1 - hi, hi)):
        terms = refs[k * count:(k + 1) * count]
        total = terms[0][...].astype(jnp.float32)
        for term in terms[1:3]:
            total = total + term[...].astype(jnp.float32)
        for term in terms[3:]:
            total = total + jnp.where(last == 1, term[...].astype(jnp.float32), 0.0)
        window = pl.ds(pl.multiple_of(place * half, half), half)
        scaled_ref[:, window] = total * g_ref[:, window]
    values = x_ref[...].astype(jnp.float32)
    centred = values - jnp.mean(values, -1, keepdims=True)
    variance = jnp.mean(centred * centred, -1, keepdims=True)
    inverse = lax.rsqrt(variance + EPSILON)
    centred = centred * inverse
    scaled = scaled_ref[...]
    corrected = inverse * (
        scaled
        - jnp.mean(scaled, -1, keepdims=True)
        - centred * jnp.mean(scaled * centred, -1, keepdims=True)
    )
    out[...] = (e_ref[...].astype(jnp.float32) + corrected).astype(out.dtype)


def own_error_of(flags, x, e, gain, far, near):
    return pl.pallas_call(
        functools.partial(own_kernel, len(far)),
        out_shape=jax.ShapeDtypeStruct(x.shape, x.dtype),
        grid_spec=pltpu.PrefetchScalarGridSpec(
            num_scalar_prefetch=1,
            grid=(1,),
            in_specs=[whole(x.shape), whole(e.shape), whole(gain.shape)]
            + [whole(t.shape) for t in (*far, *near)],
            out_specs=whole(x.shape),
            scratch_shapes=[pltpu.VMEM(x.shape, jnp.float32)],
        ),
        compiler_params=params(),
        cost_estimate=cost(20 * x.size, 16 * x.size),
    )(flags, x, e, gain, *far, *near)


def swapped(block, axis, mask):
    return lax.ppermute(block, axis, [(i, i ^ mask) for i in range(lax.axis_size(axis))])


def on_line(axis):
    return lax.axis_size(axis) == 4


def gathered(own, axis, last):
    if not on_line(axis):
        return [lax.all_gather(own, axis, axis=0, tiled=True)]
    third = swapped(own, axis, 3)
    first = swapped(own, axis, 1)
    second = lax.ppermute(
        jnp.where(last, own, third), axis, [(0, 2), (3, 1), (2, 3), (1, 0)]
    )
    return [own, first, second, third]


def returned(terms, axis, last):
    if not on_line(axis):
        return [lax.psum_scatter(terms[0], axis, scatter_dimension=0, tiled=True)]
    own, first, second, third = terms
    second = lax.ppermute(second, axis, [(2, 0), (1, 3), (3, 2), (0, 1)])
    first = swapped(first, axis, 1)
    third = swapped(
        third + jnp.where(last, jnp.zeros_like(second), second), axis, 3
    )
    return [own, first, third, second]


def summed(value, axis):
    size = lax.axis_size(axis)
    if size & (size - 1):
        return lax.psum(value, axis)
    mask = 1
    while mask < size:
        value = value + swapped(value, axis, mask)
        mask *= 2
    return value


def per_device(features, delayed_error, ln_gain, w_in, w_out):
    x, e, w_in, w_out = features[0], delayed_error[0], w_in[0], w_out[0]
    dp = lax.axis_index("dp")
    shard = lax.axis_index("shard")
    last = (shard == 0) | (shard == lax.axis_size("shard") - 1)
    hi, lo = dp // 2, dp % 2
    near = jnp.full((1,), hi, jnp.int32)
    far = 1 - near
    lo = jnp.full((1,), lo, jnp.int32)
    flags = jnp.stack([hi, last.astype(jnp.int32)])

    n_far, n_near, e_far, e_near = norm_halves(near, x, e, ln_gain)
    n_far = gathered(n_far, "shard", last)
    n_near = gathered(n_near, "shard", last)
    e_far = gathered(e_far, "shard", last)
    e_near = gathered(e_near, "shard", last)
    count = len(n_far)

    def spread(mine, for_other):
        across = swapped(for_other, "dp", 2)
        return [mine, swapped(mine, "dp", 1), across, swapped(across, "dp", 1)]

    pre, n_far = part(far, n_far, w_in, 0, "first")
    active, slope, n_near = part(near, n_near, w_in, 0, "active", (pre,))
    n_all = spread(n_near, n_far)
    active_all = spread(active, active)
    back_act, e_far = part(far, e_far, w_out, 1, "first")
    pre_error, e_near = part(near, e_near, w_out, 1, "error", (back_act, slope))
    e_all = spread(e_near, e_far)
    pre_error_all = spread(pre_error, pre_error)

    *far_terms, gain_far = back(far, count, pre_error, w_in, n_far, ln_gain)
    far_terms = returned(far_terms, "shard", last)
    *near_terms, gain_near = back(near, count, pre_error, w_in, n_near, ln_gain)
    near_terms = returned(near_terms, "shard", last)
    gain_grad = jnp.where(
        hi == 1,
        jnp.concatenate([gain_far, gain_near], 1),
        jnp.concatenate([gain_near, gain_far], 1),
    )
    gain_grad = summed(summed(gain_grad, "dp"), "shard")

    w_out_grad = grad(lo, e_all, active_all, False)
    own_error = own_error_of(flags, x, e, ln_gain, far_terms, near_terms)
    n_section = lax.axis_size("section")
    passed = lax.ppermute(
        own_error, "section", [((i + 1) % n_section, i) for i in range(n_section)]
    )
    w_in_grad = grad(lo, n_all, pre_error_all, True)
    return passed[None], gain_grad, w_in_grad[None], w_out_grad[None]


def solution(mesh):
    return jax.shard_map(
        per_device,
        mesh=mesh,
        in_specs=(
            P("section", ("dp", "shard"), None),
            P("section", ("dp", "shard"), None),
            P("section", None),
            P("section", None, "shard"),
            P("section", "shard", None),
        ),
        out_specs=(
            P("section", ("dp", "shard"), None),
            P("section", None),
            P("section", "dp", "shard"),
            P("section", "shard", "dp"),
        ),
        check_vma=False,
    )
```

```python
import functools

import jax
import jax.numpy as jnp
from jax import lax
from jax.experimental import pallas as pl
from jax.experimental.pallas import tpu as pltpu
from jax.sharding import PartitionSpec as P

SQRT_HALF = 0.7071067811865476
INV_ROOT_TWO_PI = 0.3989422804014327
EPSILON = 1e-06
MIB = 1024 * 1024
PIECES = 4


def tile_of(extent, largest=512):
    for size in (512, 384, 256, 128):
        if size <= largest and extent % size == 0:
            return size
    return extent


def dot(a, b, a_dim, b_dim):
    return lax.dot_general(
        a, b, (((a_dim,), (b_dim,)), ((), ())), preferred_element_type=jnp.float32
    )


def array(shape, kind):
    return jax.ShapeDtypeStruct(shape, kind)


def window(size, place):
    return pl.ds(pl.multiple_of(place * size, size), size)


def pair_place():
    return lax.axis_index("dp") % 2


def on_end():
    shard = lax.axis_index("shard")
    return (shard == 0) | (shard == lax.axis_size("shard") - 1)


def run(body, arrays, outputs, scratch=(), apart=(), out_apart=(), after=(), limit=None):
    n_in, n_out = len(arrays) + len(apart), len(outputs) + len(out_apart)
    anywhere, near = pl.BlockSpec(memory_space=pl.ANY), pl.BlockSpec(memory_space=pltpu.VMEM)

    def kernel(*refs):
        first = n_in + len(after)
        body(refs[:n_in], refs[first:first + n_out], refs[first + n_out:])

    return pl.pallas_call(
        kernel,
        out_shape=[*outputs, *out_apart],
        in_specs=[near] * len(arrays) + [anywhere] * (len(apart) + len(after)),
        out_specs=[near] * len(outputs) + [anywhere] * len(out_apart),
        scratch_shapes=list(scratch),
        compiler_params=pltpu.CompilerParams(
            vmem_limit_bytes=((limit or 8) if lax.axis_size("shard") == 4 else 58) * MIB
        ),
        cost_estimate=pl.CostEstimate(flops=1000, bytes_accessed=1000, transcendentals=0),
    )(*arrays, *apart, *after)


def normalised(x_ref):
    values = x_ref[...].astype(jnp.float32)
    centred = values - jnp.mean(values, -1, keepdims=True)
    variance = jnp.mean(centred * centred, -1, keepdims=True)
    inverse = lax.rsqrt(variance + EPSILON)
    return centred * inverse, inverse


def far_place():
    return 1 - lax.axis_index("dp") // 2


def near_place():
    return lax.axis_index("dp") // 2


def tokens_of(x, e, gain):
    rows, width = x.shape
    half = width // 2

    def body(ins, outs, scratch):
        x_near, e_near, g_near, sems = scratch
        copies = [
            pltpu.make_async_copy(ins[k], place, sems.at[k])
            for k, place in enumerate((x_near, e_near, g_near))
        ]
        for copy in copies:
            copy.start()
        for copy in copies:
            copy.wait()
        outs[0][:rows, :] = (normalised(x_near)[0] * g_near[...]).astype(x.dtype)
        outs[0][rows:, :] = e_near[...]
        outs[1][...] = outs[0][:, window(half, far_place())]

    return run(
        body, (), [array((2 * rows, width), x.dtype), array((2 * rows, half), x.dtype)],
        apart=(x, e, gain),
        scratch=[
            pltpu.VMEM(x.shape, x.dtype),
            pltpu.VMEM(e.shape, e.dtype),
            pltpu.VMEM(gain.shape, gain.dtype),
            pltpu.SemaphoreType.DMA((3,)),
        ],
        limit=58,
    )


def passed_on(own, came, after=()):
    rows, width = own.shape
    half = width // 2

    def body(ins, outs, scratch):
        for out, place in zip(outs, (far_place(), near_place())):
            columns = window(half, place)
            out[...] = jnp.where(on_end(), ins[0][:, columns], ins[1][:, columns])

    return run(body, (own, came), [array((rows, half), own.dtype)] * 2, after=after)


def far_of(block, after=()):
    rows, width = block.shape
    half = width // 2

    def body(ins, outs, scratch):
        outs[0][...] = ins[0][:, window(half, far_place())]

    return run(body, (block,), [array((rows, half), block.dtype)], after=after)[0]


def grouped(blocks, near, apart=(), pieces=0, after=()):
    half = blocks[0].shape[1] // 2
    rows, kind = blocks[0].shape[0] // 2, blocks[0].dtype
    below = rows * len(blocks)

    def body(ins, outs, scratch):
        columns = window(half, near_place() if near else far_place())
        for k, block in enumerate(ins):
            part = block[...] if block.shape[1] == half else block[:, columns]
            outs[0][k * rows:(k + 1) * rows, :] = part[:rows]
            outs[0][below + k * rows:below + (k + 1) * rows, :] = part[rows:]
            if k in apart:
                at = apart.index(k) * 2 * rows
                outs[1][at:at + 2 * rows, :] = part
        for k in range(pieces):
            at = k * (2 * below // pieces)
            outs[1 + k][...] = outs[0][at:at + 2 * below // pieces, :]

    outs = [array((2 * below, half), kind)]
    if apart:
        outs.append(array((2 * rows * len(apart), half), kind))
    outs += [array((2 * below // pieces, half), kind)] * pieces if pieces else []
    return run(body, blocks, outs, after=after)


def regrouped(parts, after=()):
    half = parts[0].shape[1]
    rows = parts[0].shape[0] // 2
    count = sum(part.shape[0] for part in parts) // (2 * rows)

    def body(ins, outs, scratch):
        blocks = [
            part[at:at + 2 * rows, :] for part in ins for at in range(0, part.shape[0], 2 * rows)
        ]
        for k, block in enumerate(blocks):
            outs[0][k * rows:(k + 1) * rows, :] = block[:rows]
            outs[0][(count + k) * rows:(count + k + 1) * rows, :] = block[rows:]

    outs = [array((2 * count * rows, half), parts[0].dtype)]
    return run(body, parts, outs, after=after)[0]


def held(block, after):
    def body(ins, outs, scratch):
        outs[0][...] = ins[0][...]

    return run(body, (block,), [array(block.shape, block.dtype)], after=after)[0]


def forth_and_back(groups, w_in, w_out, after=()):
    tokens, half = groups[0].shape
    rows, hidden, kind = tokens // 2, w_in.shape[1] // 2, groups[0].dtype
    tile = tile_of(hidden)
    steps = hidden // tile

    def body(ins, outs, scratch):
        w_in_ref, w_out_ref = ins[-2:]
        rows_all, in_weight, out_weight, sems = scratch

        def coming(j, forth, near=False):
            units = window(tile, pair_place() * steps + j)
            place = window(tile, j)
            depth = window(half, near_place() if near else far_place())
            if forth:
                source = w_in_ref.at[depth, units]
                target = (outs[2] if near else in_weight).at[:, place]
            else:
                source = w_out_ref.at[units, depth]
                target = (outs[3] if near else out_weight).at[place, :]
            return pltpu.make_async_copy(
                source, target, sems.at[2 * int(near) + 1 - int(forth), j]
            )

        every = [(j, forth, near) for near in (False, True) for forth in (True, False) for j in range(steps)]
        for which in every:
            coming(*which).start()
        for k in range(2):
            rows_all[k * rows:(k + 1) * rows, :] = ins[k][:rows, :]

        @pl.loop(0, steps)
        def _(j):
            coming(j, True).wait()
            place = window(tile, j)
            outs[0][:, place] = dot(rows_all[...], in_weight[:, place], 1, 0)

        for k in range(2):
            rows_all[k * rows:(k + 1) * rows, :] = ins[k][rows:, :]

        @pl.loop(0, steps)
        def _(j):
            coming(j, False).wait()
            place = window(tile, j)
            outs[1][:, place] = dot(rows_all[...], out_weight[place, :], 1, 1)

        for which in every[2 * steps:]:
            coming(*which).wait()

    wide = array((tokens, hidden), jnp.float32)
    return run(
        body, groups,
        [wide, wide, array((half, hidden), kind), array((hidden, half), kind)],
        apart=(w_in, w_out),
        scratch=[
            pltpu.VMEM((tokens, half), kind),
            pltpu.VMEM((half, hidden), kind),
            pltpu.VMEM((hidden, half), kind),
            pltpu.SemaphoreType.DMA((4, steps)),
        ],
        after=after, limit=24,
    )


def finished(group, pairs, prior, after=()):
    tokens, half = group.shape
    rows, hidden, kind = tokens // 2, prior[0].shape[1], group.dtype
    tile = tile_of(hidden)
    piece = pairs[0].shape[0]
    each = rows // piece

    def body(ins, outs, scratch):
        pre_ref, back_act_ref, in_weight, out_weight = ins[1 + 2 * each:]
        rows_all, slope_ref = scratch

        def stack(below):
            rows_all[:rows, :] = ins[0][below * rows:(below + 1) * rows, :]
            for k in range(each):
                at = rows + k * piece
                rows_all[at:at + piece, :] = ins[1 + below * each + k][...]

        stack(0)

        @pl.loop(0, hidden // tile)
        def _(j):
            place = window(tile, j)
            pre = pre_ref[:, place] + dot(rows_all[...], in_weight[:, place], 1, 0)
            normal_cdf = 0.5 * (1.0 + lax.erf(pre * SQRT_HALF))
            density = INV_ROOT_TWO_PI * jnp.exp(-0.5 * pre * pre)
            outs[0][:tokens, place] = (pre * normal_cdf).astype(kind)
            slope_ref[:, place] = normal_cdf + pre * density

        stack(1)

        @pl.loop(0, hidden // tile)
        def _(j):
            place = window(tile, j)
            back_act = back_act_ref[:, place] + dot(rows_all[...], out_weight[place, :], 1, 1)
            outs[0][tokens:, place] = (back_act * slope_ref[:, place]).astype(kind)

    return run(
        body, (group, *pairs, *prior), [array((2 * tokens, hidden), kind)],
        [pltpu.VMEM((tokens, half), kind), pltpu.VMEM((tokens, hidden), jnp.float32)],
        after=after, limit=8,
    )[0]


def sums(both, near_weight, w_in, after=()):
    tokens, hidden = both.shape[0] // 2, both.shape[1]
    half, rows, kind = near_weight.shape[0], tokens // 2, both.dtype
    tile = tile_of(half)
    piece = rows // PIECES

    def body(ins, outs, scratch):
        far_weight, sem = scratch
        coming = pltpu.make_async_copy(
            ins[2].at[window(half, far_place()), window(hidden, pair_place())], far_weight, sem
        )
        coming.start()
        for weight, place in ((ins[1], near_place()), (far_weight, far_place())):
            first = place * (half // tile)
            if weight is far_weight:
                coming.wait()

            @pl.loop(0, half // tile)
            def _(j):
                columns = window(tile, first + j)
                term = dot(ins[0][tokens:, :], weight[window(tile, j), :], 1, 1)
                outs[0][:, columns] = term[:rows]
                for k in range(PIECES):
                    at = rows + k * piece
                    outs[1 + k][:, columns] = term[at:at + piece].astype(kind)

    return run(
        body, (both, near_weight),
        [array((rows, 2 * half), jnp.float32)] + [array((piece, 2 * half), kind)] * PIECES,
        [pltpu.VMEM((half, hidden), kind), pltpu.SemaphoreType.DMA],
        apart=(w_in,), after=after, limit=16,
    )


def joined(mine, others, far, near, gain, count, after=()):
    rows, width = mine.shape
    half = width // 2
    block = rows // count
    kind = others[0].dtype
    piece = rows // PIECES

    def body(ins, outs, scratch):
        mine_ref, others_ref, g_ref = ins[0], ins[1:1 + PIECES], ins[-1]
        for group_ref, place in ((ins[-3], far_place()), (ins[-2], near_place())):
            columns = window(half, place)
            total = jnp.zeros((1, half), jnp.float32)
            for k in range(PIECES):
                here = slice(k * piece, (k + 1) * piece)
                term = mine_ref[here, columns] + others_ref[k][:, columns].astype(jnp.float32)
                term = term.astype(kind)
                if count == PIECES:
                    outs[k][:, columns] = term
                else:
                    outs[0][here, columns] = term
                weighed = term.astype(jnp.float32) * group_ref[here, :].astype(jnp.float32)
                total = total + jnp.sum(weighed, 0, keepdims=True)
            outs[count][:, columns] = total / g_ref[:, columns]

    return run(
        body, (mine, *others, far, near, gain),
        [array((block, width), kind)] * count + [array((1, width), jnp.float32)],
        after=after,
    )


def added(mine, came, after=()):
    def body(ins, outs, scratch):
        came_here = jnp.where(on_end(), 0.0, ins[1][...].astype(jnp.float32))
        outs[0][...] = (ins[0][...].astype(jnp.float32) + came_here).astype(mine.dtype)

    return run(body, (mine, came), [array(mine.shape, mine.dtype)], after=after)[0]


def gradients(cut, full, after=()):
    tokens, part = full[0].shape[0] // 2, full[0].shape[1]
    rows, width, kind = tokens // 2, cut[0][0].shape[1] // 2, full[0].dtype
    tile = tile_of(2 * part)
    steps = 2 * part // tile
    names = [entry[0] for entry in cut]

    def body(ins, outs, scratch):
        a_all, b_all, wide, tall, in_sems, sems = scratch
        lo = pair_place()
        moves = [[], []]
        for which in range(2):
            at = 0
            for k, (_, first, count) in enumerate(cut):
                if first[which] is None:
                    continue
                source = ins[k].at[pl.ds(first[which], count), window(width, lo)]
                moves[which].append((source, a_all.at[which, pl.ds(at, count), :]))
                at += count
            for k in range(4):
                for half in range(2):
                    at = (k // 2 * 2 + (half if k % 2 == 0 else 1 - half)) * rows
                    place = window(part, lo if k % 2 == 0 else 1 - lo)
                    source = ins[len(cut) + k].at[pl.ds(which * tokens + half * rows, rows), :]
                    moves[which].append((source, b_all.at[which, pl.ds(at, rows), place]))
        copies = [
            [
                pltpu.make_async_copy(a, b, in_sems.at[which, k])
                for k, (a, b) in enumerate(moves[which])
            ]
            for which in range(2)
        ]
        for copy in [*copies[0], *copies[1]]:
            copy.start()

        for which in range(2):
            for copy in copies[which]:
                copy.wait()
            buffer = (tall, wide)[which]

            def leaving(j):
                place = window(tile, j)
                target = outs[1 + which].at[place, :] if which == 0 else outs[1 + which].at[:, place]
                return pltpu.make_async_copy(buffer.at[j % 2], target, sems.at[which, j % 2])

            @pl.loop(0, steps)
            def _(j):
                place = window(tile, j)
                if which == 0:
                    result = dot(b_all[0, :, place], a_all[0], 0, 0)
                else:
                    result = dot(a_all[1], b_all[1, :, place], 0, 0)

                @pl.when(j >= 2)
                def _():
                    leaving(j - 2).wait()

                buffer[j % 2] = result.astype(kind)
                leaving(j).start()

            if which == 1:
                for k in range(2):
                    buffer = (tall, wide)[k]
                    for j in range(max(steps - 2, 0), steps):
                        place = window(tile, j)
                        target = outs[1 + k].at[place, :] if k == 0 else outs[1 + k].at[:, place]
                        pltpu.make_async_copy(
                            buffer.at[j % 2], target, sems.at[k, j % 2]
                        ).wait()
        outs[0][...] = jnp.zeros_like(outs[0])

    return run(
        body, (), [array((8, 128), jnp.float32)],
        out_apart=[array((2 * part, width), kind), array((width, 2 * part), kind)],
        apart=[*names, *full],
        scratch=[
            pltpu.VMEM((2, 4 * rows, width), kind),
            pltpu.VMEM((2, 4 * rows, 2 * part), kind),
            pltpu.VMEM((2, width, tile), kind),
            pltpu.VMEM((2, tile, width), kind),
            pltpu.SemaphoreType.DMA((2, len(cut) + 8)),
            pltpu.SemaphoreType.DMA((2, 2)),
        ],
        after=after, limit=24,
    )


def total(parts, after=()):
    def body(ins, outs, scratch):
        sums = [part[...] for part in ins]
        while len(sums) > 1:
            sums = [sums[k] + sums[k + 1] for k in range(0, len(sums), 2)]
        outs[0][...] = sums[0]

    return run(body, parts, [array(parts[0].shape, parts[0].dtype)], after=after)[0]


def own_error_of(x, e, gain, terms, after=()):
    def body(ins, outs, scratch):
        x_ref, e_ref, g_ref = ins[:3]
        total = ins[3][...].astype(jnp.float32)
        for term in ins[4:6]:
            total = total + term[...].astype(jnp.float32)
        for term in ins[6:]:
            total = total + jnp.where(on_end(), term[...].astype(jnp.float32), 0.0)
        scaled = total * g_ref[...]
        centred, inverse = normalised(x_ref)
        corrected = inverse * (
            scaled
            - jnp.mean(scaled, -1, keepdims=True)
            - centred * jnp.mean(scaled * centred, -1, keepdims=True)
        )
        outs[0][...] = (e_ref[...].astype(jnp.float32) + corrected).astype(x.dtype)

    return run(body, (x, e, gain, *terms), [array(x.shape, x.dtype)], after=after)[0]


def swapped(block, axis, mask):
    return lax.ppermute(block, axis, [(i, i ^ mask) for i in range(lax.axis_size(axis))])


def pair(block):
    return swapped(block, "dp", 1)


def across(block):
    return swapped(block, "dp", 2)


def summed(value, axis):
    size = lax.axis_size(axis)
    if size & (size - 1):
        return lax.psum(value, axis)
    mask = 1
    while mask < size:
        value = value + swapped(value, axis, mask)
        mask *= 2
    return value


RELAY = [(0, 2), (3, 1), (2, 3), (1, 0)]
RELAY_BACK = [(b, a) for a, b in RELAY]


def gathered(chunk):
    return [
        lax.all_gather(chunk, "shard", axis=0)[k] for k in range(lax.axis_size("shard"))
    ]


def per_device(features, delayed_error, ln_gain, w_in, w_out):
    x, e, w_in, w_out = features[0], delayed_error[0], w_in[0], w_out[0]
    line = lax.axis_size("shard") == 4

    own, own_far = tokens_of(x, e, ln_gain)
    if line:
        first, third = swapped(own, "shard", 1), swapped(own, "shard", 3)
        own_across = across(own_far)
        passing_far, passing_near = passed_on(own, third, after=(own_across,))
        second_far = lax.ppermute(passing_far, "shard", RELAY)
        second_near = lax.ppermute(passing_near, "shard", RELAY)
        first_across = across(far_of(first))
        blocks = [own, first, second_far, third]
        far, rest_far = grouped(blocks, False, apart=(2, 3), after=(first_across,))
        rest_across = across(rest_far)
        blocks = [own, first, second_near, third]
        tie = (rest_across,)
    else:
        blocks = gathered(own)
        (far,) = grouped(blocks, False)
        far_across = across(far)
        tie = ()
    far_pair = pair(far)
    prior = forth_and_back((far, far_pair), w_in, w_out)
    near, *pieces = grouped(blocks, True, pieces=PIECES, after=(prior[0],))
    pairs = [pair(piece) for piece in pieces]
    both = finished(near, pairs, prior, after=tie)
    both_across = across(both)
    both_pair = pair(both)
    mine, *others = sums(both, prior[2], w_in)
    if line:
        far_across = regrouped((own_across, first_across, rest_across), after=(others[0],))
    count = PIECES if line else 1
    *terms, gain_grad = joined(
        mine, [pair(other) for other in others], far, near, ln_gain, count
    )
    if line:
        own_terms, first_terms, second_terms, third_terms = terms
        second_terms = lax.ppermute(second_terms, "shard", RELAY_BACK)
        first_terms = swapped(first_terms, "shard", 1)
        passing = added(third_terms, second_terms, after=(both_pair,))
        tie = (passing,)
        terms = [own_terms, first_terms, swapped(passing, "shard", 3), second_terms]
        tie = (terms[1], terms[2])
        far_across = held(far_across, (passing,))
        gain_grad = held(gain_grad, (passing,))
    else:
        terms = [lax.psum_scatter(terms[0], "shard", scatter_dimension=0, tiled=True)]
    far_across_pair = pair(far_across)
    both_across = held(both_across, tie)
    both_across_pair = pair(both_across)
    own_error = own_error_of(x, e, ln_gain, terms, after=(both_across,))
    n_section = lax.axis_size("section")
    passed = lax.ppermute(
        own_error, "section", [((i + 1) % n_section, i) for i in range(n_section)]
    )
    gain_grad = held(summed(gain_grad, "dp"), (own_error,))
    if line:
        gain_parts = [gain_grad] + [swapped(gain_grad, "shard", mask) for mask in (1, 2, 3)]
    else:
        gain_parts = [summed(gain_grad, "shard")]

    tokens = both.shape[0] // 2
    rows = tokens // 2
    piece = pairs[0].shape[0]
    each = rows // piece
    cut = [(near, (rows, 0), rows)]
    cut += [(pairs[k], (None, 0) if k < each else (0, None), piece) for k in range(PIECES)]
    cut += [(far_across, (rows, 0), rows), (far_across_pair, (rows, 0), rows)]
    token, w_out_grad, w_in_grad = gradients(
        cut, (both, both_pair, both_across, both_across_pair), after=(own_error,)
    )
    gain_grad = total(gain_parts, after=(token,))
    return passed[None], gain_grad, w_in_grad[None], w_out_grad[None]


def solution(mesh):
    return jax.shard_map(
        per_device,
        mesh=mesh,
        in_specs=(
            P("section", ("dp", "shard"), None),
            P("section", ("dp", "shard"), None),
            P("section", None),
            P("section", None, "shard"),
            P("section", "shard", None),
        ),
        out_specs=(
            P("section", ("dp", "shard"), None),
            P("section", None),
            P("section", "dp", "shard"),
            P("section", "shard", "dp"),
        ),
        check_vma=False,
    )
```

```python
import functools

import jax
import jax.numpy as jnp
from jax import lax
from jax.experimental import pallas as pl
from jax.experimental.pallas import tpu as pltpu
from jax.sharding import PartitionSpec as P

SQRT_HALF = 0.7071067811865476
INV_ROOT_TWO_PI = 0.3989422804014327
EPSILON = 1e-06
MIB = 1024 * 1024
PIECES = 4


def tile_of(extent, largest=512):
    for size in (512, 384, 256, 128):
        if size <= largest and extent % size == 0:
            return size
    return extent


def dot(a, b, a_dim, b_dim):
    return lax.dot_general(
        a, b, (((a_dim,), (b_dim,)), ((), ())), preferred_element_type=jnp.float32
    )


def array(shape, kind):
    return jax.ShapeDtypeStruct(shape, kind)


def window(size, place):
    return pl.ds(pl.multiple_of(place * size, size), size)


def pair_place():
    return lax.axis_index("dp") % 2


def on_end():
    shard = lax.axis_index("shard")
    return (shard == 0) | (shard == lax.axis_size("shard") - 1)


def run(body, arrays, outputs, scratch=(), apart=(), out_apart=(), after=(), limit=None):
    n_in, n_out = len(arrays) + len(apart), len(outputs) + len(out_apart)
    anywhere, near = pl.BlockSpec(memory_space=pl.ANY), pl.BlockSpec(memory_space=pltpu.VMEM)

    def kernel(*refs):
        first = n_in + len(after)
        body(refs[:n_in], refs[first:first + n_out], refs[first + n_out:])

    return pl.pallas_call(
        kernel,
        out_shape=[*outputs, *out_apart],
        in_specs=[near] * len(arrays) + [anywhere] * (len(apart) + len(after)),
        out_specs=[near] * len(outputs) + [anywhere] * len(out_apart),
        scratch_shapes=list(scratch),
        compiler_params=pltpu.CompilerParams(
            vmem_limit_bytes=((limit or 8) if lax.axis_size("shard") == 4 else 58) * MIB
        ),
        cost_estimate=pl.CostEstimate(flops=1000, bytes_accessed=1000, transcendentals=0),
    )(*arrays, *apart, *after)


def normalised(x_ref):
    values = x_ref[...].astype(jnp.float32)
    centred = values - jnp.mean(values, -1, keepdims=True)
    variance = jnp.mean(centred * centred, -1, keepdims=True)
    inverse = lax.rsqrt(variance + EPSILON)
    return centred * inverse, inverse


def far_place():
    return 1 - lax.axis_index("dp") // 2


def near_place():
    return lax.axis_index("dp") // 2


def tokens_of(x, e, gain):
    rows, width = x.shape
    half = width // 2

    def body(ins, outs, scratch):
        x_near, e_near, g_near, sems = scratch
        copies = [
            pltpu.make_async_copy(ins[k], place, sems.at[k])
            for k, place in enumerate((x_near, e_near, g_near))
        ]
        for copy in copies:
            copy.start()
        for copy in copies:
            copy.wait()
        outs[0][:rows, :] = (normalised(x_near)[0] * g_near[...]).astype(x.dtype)
        outs[0][rows:, :] = e_near[...]
        outs[1][...] = outs[0][:, window(half, far_place())]

    return run(
        body, (), [array((2 * rows, width), x.dtype), array((2 * rows, half), x.dtype)],
        apart=(x, e, gain),
        scratch=[
            pltpu.VMEM(x.shape, x.dtype),
            pltpu.VMEM(e.shape, e.dtype),
            pltpu.VMEM(gain.shape, gain.dtype),
            pltpu.SemaphoreType.DMA((3,)),
        ],
        limit=58,
    )


def passed_on(own, came, after=()):
    rows, width = own.shape
    half = width // 2

    def body(ins, outs, scratch):
        for out, place in zip(outs, (far_place(), near_place())):
            columns = window(half, place)
            out[...] = jnp.where(on_end(), ins[0][:, columns], ins[1][:, columns])

    return run(body, (own, came), [array((rows, half), own.dtype)] * 2, after=after)


def far_of(block, after=()):
    rows, width = block.shape
    half = width // 2

    def body(ins, outs, scratch):
        outs[0][...] = ins[0][:, window(half, far_place())]

    return run(body, (block,), [array((rows, half), block.dtype)], after=after)[0]


def grouped(blocks, near, apart=(), pieces=0, after=()):
    half = blocks[0].shape[1] // 2
    rows, kind = blocks[0].shape[0] // 2, blocks[0].dtype
    below = rows * len(blocks)

    def body(ins, outs, scratch):
        columns = window(half, near_place() if near else far_place())
        for k, block in enumerate(ins):
            part = block[...] if block.shape[1] == half else block[:, columns]
            outs[0][k * rows:(k + 1) * rows, :] = part[:rows]
            outs[0][below + k * rows:below + (k + 1) * rows, :] = part[rows:]
            if k in apart:
                at = apart.index(k) * 2 * rows
                outs[1][at:at + 2 * rows, :] = part
        for k in range(pieces):
            at = k * (2 * below // pieces)
            outs[1 + k][...] = outs[0][at:at + 2 * below // pieces, :]

    outs = [array((2 * below, half), kind)]
    if apart:
        outs.append(array((2 * rows * len(apart), half), kind))
    outs += [array((2 * below // pieces, half), kind)] * pieces if pieces else []
    return run(body, blocks, outs, after=after)


def regrouped(blocks, folded, after=()):
    rows, half = blocks[0].shape
    rows //= 2
    count = len(blocks) + 1
    hidden = folded.shape[1]
    first = folded.shape[0] - half // hidden * 2 * rows

    def body(ins, outs, scratch):
        for k, block in enumerate(ins[:-1]):
            outs[0][k * rows:(k + 1) * rows, :] = block[:rows, :]
            outs[0][(count + k) * rows:(count + k + 1) * rows, :] = block[rows:, :]
        for j in range(half // hidden):
            at = first + j * 2 * rows
            columns = slice(j * hidden, (j + 1) * hidden)
            outs[0][(count - 1) * rows:count * rows, columns] = ins[-1][at:at + rows, :]
            outs[0][(2 * count - 1) * rows:, columns] = ins[-1][at + rows:at + 2 * rows, :]

    outs = [array((2 * count * rows, half), blocks[0].dtype)]
    return run(body, (*blocks, folded), outs, after=after)[0]


def held(block, after):
    def body(ins, outs, scratch):
        outs[0][...] = ins[0][...]

    return run(body, (block,), [array(block.shape, block.dtype)], after=after)[0]


def forth_and_back(groups, w_in, w_out, after=()):
    tokens, half = groups[0].shape
    rows, hidden, kind = tokens // 2, w_in.shape[1] // 2, groups[0].dtype
    tile = tile_of(hidden)
    steps = hidden // tile

    def body(ins, outs, scratch):
        w_in_ref, w_out_ref = ins[-2:]
        rows_all, in_weight, out_weight, sems, near_sem = scratch

        def coming(j, forth):
            units = window(tile, pair_place() * steps + j)
            place, depth = window(tile, j), window(half, far_place())
            if forth:
                source, target = w_in_ref.at[depth, units], in_weight.at[:, place]
            else:
                source, target = w_out_ref.at[units, depth], out_weight.at[place, :]
            return pltpu.make_async_copy(source, target, sems.at[1 - int(forth), j])

        along = pltpu.make_async_copy(
            w_in_ref.at[window(half, near_place()), window(hidden, pair_place())],
            outs[2], near_sem,
        )
        for forth in (True, False):
            for j in range(steps):
                coming(j, forth).start()
        along.start()
        for k in range(2):
            rows_all[k * rows:(k + 1) * rows, :] = ins[k][:rows, :]

        @pl.loop(0, steps)
        def _(j):
            coming(j, True).wait()
            place = window(tile, j)
            outs[0][:, place] = dot(rows_all[...], in_weight[:, place], 1, 0)

        for k in range(2):
            rows_all[k * rows:(k + 1) * rows, :] = ins[k][rows:, :]

        @pl.loop(0, steps)
        def _(j):
            coming(j, False).wait()
            place = window(tile, j)
            outs[1][:, place] = dot(rows_all[...], out_weight[place, :], 1, 1)

        along.wait()

    wide = array((tokens, hidden), jnp.float32)
    return run(
        body, groups, [wide, wide, array((half, hidden), kind)], apart=(w_in, w_out),
        scratch=[
            pltpu.VMEM((tokens, half), kind),
            pltpu.VMEM((half, hidden), kind),
            pltpu.VMEM((hidden, half), kind),
            pltpu.SemaphoreType.DMA((2, steps)),
            pltpu.SemaphoreType.DMA,
        ],
        after=after, limit=24,
    )


def finished(group, pairs, prior, w_out, along=(), after=()):
    tokens, half = group.shape
    rows, hidden, kind = tokens // 2, prior[0].shape[1], group.dtype
    tile = tile_of(hidden)
    steps = hidden // tile
    piece = pairs[0].shape[0]
    each = rows // piece

    def body(ins, outs, scratch):
        pre_ref, back_act_ref, in_weight, *more, w_out_ref = ins[1 + 2 * each:]
        rows_all, slope_ref, out_weight, sems = scratch

        def coming(j):
            units = window(tile, pair_place() * steps + j)
            return pltpu.make_async_copy(
                w_out_ref.at[units, window(half, near_place())],
                out_weight.at[window(tile, j), :],
                sems.at[j],
            )

        for j in range(steps):
            coming(j).start()

        def stack(below):
            rows_all[:rows, :] = ins[0][below * rows:(below + 1) * rows, :]
            for k in range(each):
                at = rows + k * piece
                rows_all[at:at + piece, :] = ins[1 + below * each + k][...]

        for block in more:
            for k in range(half // hidden):
                at = tokens + k * block.shape[0]
                outs[0][at:at + block.shape[0], :] = block[:, k * hidden:(k + 1) * hidden]
        stack(0)

        @pl.loop(0, steps)
        def _(j):
            place = window(tile, j)
            pre = pre_ref[:, place] + dot(rows_all[...], in_weight[:, place], 1, 0)
            normal_cdf = 0.5 * (1.0 + lax.erf(pre * SQRT_HALF))
            density = INV_ROOT_TWO_PI * jnp.exp(-0.5 * pre * pre)
            active = (pre * normal_cdf).astype(kind)
            outs[0][:tokens, place] = active
            outs[2][:tokens, place] = active
            slope_ref[:, place] = normal_cdf + pre * density

        stack(1)

        @pl.loop(0, steps)
        def _(j):
            coming(j).wait()
            place = window(tile, j)
            back_act = back_act_ref[:, place] + dot(rows_all[...], out_weight[place, :], 1, 1)
            pre_error = (back_act * slope_ref[:, place]).astype(kind)
            outs[1][:, place] = pre_error
            outs[2][tokens:, place] = pre_error

    below = sum(block.size // hidden for block in along)
    return run(
        body, (group, *pairs, *prior, *along),
        [array((rows, hidden), kind) for rows in (tokens + below, tokens, 2 * tokens)],
        [
            pltpu.VMEM((tokens, half), kind),
            pltpu.VMEM((tokens, hidden), jnp.float32),
            pltpu.VMEM((hidden, half), kind),
            pltpu.SemaphoreType.DMA((steps,)),
        ],
        apart=(w_out,), after=after, limit=18,
    )


def sums(pre_error, near_weight, w_in, after=()):
    tokens, hidden = pre_error.shape
    half, rows, kind = near_weight.shape[0], tokens // 2, pre_error.dtype
    tile = tile_of(half)
    piece = rows // PIECES

    def body(ins, outs, scratch):
        far_weight, sem = scratch
        coming = pltpu.make_async_copy(
            ins[2].at[window(half, far_place()), window(hidden, pair_place())], far_weight, sem
        )
        coming.start()
        for weight, place in ((ins[1], near_place()), (far_weight, far_place())):
            first = place * (half // tile)
            if weight is far_weight:
                coming.wait()

            @pl.loop(0, half // tile)
            def _(j):
                columns = window(tile, first + j)
                term = dot(ins[0][...], weight[window(tile, j), :], 1, 1)
                outs[0][:, columns] = term[:rows]
                for k in range(PIECES):
                    at = rows + k * piece
                    outs[1 + k][:, columns] = term[at:at + piece].astype(kind)

    return run(
        body, (pre_error, near_weight),
        [array((rows, 2 * half), jnp.float32)] + [array((piece, 2 * half), kind)] * PIECES,
        [pltpu.VMEM((half, hidden), kind), pltpu.SemaphoreType.DMA],
        apart=(w_in,), after=after, limit=16,
    )


def joined(mine, others, far, near, gain, count, after=()):
    rows, width = mine.shape
    half = width // 2
    block = rows // count
    kind = others[0].dtype
    piece = rows // PIECES

    def body(ins, outs, scratch):
        mine_ref, others_ref, g_ref = ins[0], ins[1:1 + PIECES], ins[-1]
        for group_ref, place in ((ins[-3], far_place()), (ins[-2], near_place())):
            columns = window(half, place)
            total = jnp.zeros((1, half), jnp.float32)
            for k in range(PIECES):
                here = slice(k * piece, (k + 1) * piece)
                term = mine_ref[here, columns] + others_ref[k][:, columns].astype(jnp.float32)
                term = term.astype(kind)
                if count == PIECES:
                    outs[k][:, columns] = term
                else:
                    outs[0][here, columns] = term
                weighed = term.astype(jnp.float32) * group_ref[here, :].astype(jnp.float32)
                total = total + jnp.sum(weighed, 0, keepdims=True)
            outs[count][:, columns] = total / g_ref[:, columns]

    return run(
        body, (mine, *others, far, near, gain),
        [array((block, width), kind)] * count + [array((1, width), jnp.float32)],
        after=after,
    )


def added(mine, came, after=()):
    def body(ins, outs, scratch):
        came_here = jnp.where(on_end(), 0.0, ins[1][...].astype(jnp.float32))
        outs[0][...] = (ins[0][...].astype(jnp.float32) + came_here).astype(mine.dtype)

    return run(body, (mine, came), [array(mine.shape, mine.dtype)], after=after)[0]


def gradient(cut, full, rows, cut_rows, after=()):
    part, width, kind = full[0][0].shape[1], cut[0][0].shape[1] // 2, full[0][0].dtype
    tile = tile_of(2 * part)
    steps = 2 * part // tile
    shape = (width, 2 * part) if cut_rows else (2 * part, width)

    def body(ins, outs, scratch):
        a_all, b_all, buffer, in_sems, sems = scratch
        lo = pair_place()
        moves, at = [], 0
        for k, (_, first, count) in enumerate(cut):
            source = ins[k].at[pl.ds(first, count), window(width, lo)]
            moves.append((source, a_all.at[pl.ds(at, count), :]))
            at += count
        for k, (_, first) in enumerate(full):
            for half in range(2):
                at = (k // 2 * 2 + (half if k % 2 == 0 else 1 - half)) * rows
                place = window(part, lo if k % 2 == 0 else 1 - lo)
                source = ins[len(cut) + k].at[pl.ds(first + half * rows, rows), :]
                moves.append((source, b_all.at[pl.ds(at, rows), place]))
        copies = [
            pltpu.make_async_copy(a, b, in_sems.at[k]) for k, (a, b) in enumerate(moves)
        ]
        for copy in copies:
            copy.start()
        for copy in copies:
            copy.wait()

        def leaving(j):
            place = window(tile, j)
            target = outs[1].at[:, place] if cut_rows else outs[1].at[place, :]
            return pltpu.make_async_copy(buffer.at[j % 2], target, sems.at[j % 2])

        @pl.loop(0, steps)
        def _(j):
            place = window(tile, j)
            if cut_rows:
                result = dot(a_all[...], b_all[:, place], 0, 0)
            else:
                result = dot(b_all[:, place], a_all[...], 0, 0)

            @pl.when(j >= 2)
            def _():
                leaving(j - 2).wait()

            buffer[j % 2] = result.astype(kind)
            leaving(j).start()

        for j in range(max(steps - 2, 0), steps):
            leaving(j).wait()
        outs[0][...] = jnp.zeros_like(outs[0])

    return run(
        body, (), [array((8, 128), jnp.float32)], out_apart=[array(shape, kind)],
        apart=[a for a, *_ in (*cut, *full)],
        scratch=[
            pltpu.VMEM((4 * rows, width), kind),
            pltpu.VMEM((4 * rows, 2 * part), kind),
            pltpu.VMEM((2, width, tile) if cut_rows else (2, tile, width), kind),
            pltpu.SemaphoreType.DMA((len(cut) + 8,)),
            pltpu.SemaphoreType.DMA((2,)),
        ],
        after=after, limit=16,
    )


def total(parts, after=()):
    def body(ins, outs, scratch):
        sums = [part[...] for part in ins]
        while len(sums) > 1:
            sums = [sums[k] + sums[k + 1] for k in range(0, len(sums), 2)]
        outs[0][...] = sums[0]

    return run(body, parts, [array(parts[0].shape, parts[0].dtype)], after=after)[0]


def own_error_of(x, e, gain, terms, after=()):
    def body(ins, outs, scratch):
        x_ref, e_ref, g_ref = ins[:3]
        total = ins[3][...].astype(jnp.float32)
        for term in ins[4:6]:
            total = total + term[...].astype(jnp.float32)
        for term in ins[6:]:
            total = total + jnp.where(on_end(), term[...].astype(jnp.float32), 0.0)
        scaled = total * g_ref[...]
        centred, inverse = normalised(x_ref)
        corrected = inverse * (
            scaled
            - jnp.mean(scaled, -1, keepdims=True)
            - centred * jnp.mean(scaled * centred, -1, keepdims=True)
        )
        outs[0][...] = (e_ref[...].astype(jnp.float32) + corrected).astype(x.dtype)

    return run(body, (x, e, gain, *terms), [array(x.shape, x.dtype)], after=after)[0]


def swapped(block, axis, mask):
    return lax.ppermute(block, axis, [(i, i ^ mask) for i in range(lax.axis_size(axis))])


def pair(block):
    return swapped(block, "dp", 1)


def across(block):
    return swapped(block, "dp", 2)


def summed(value, axis):
    size = lax.axis_size(axis)
    if size & (size - 1):
        return lax.psum(value, axis)
    mask = 1
    while mask < size:
        value = value + swapped(value, axis, mask)
        mask *= 2
    return value


RELAY = [(0, 2), (3, 1), (2, 3), (1, 0)]
RELAY_BACK = [(b, a) for a, b in RELAY]


def gathered(chunk):
    return [
        lax.all_gather(chunk, "shard", axis=0)[k] for k in range(lax.axis_size("shard"))
    ]


def per_device(features, delayed_error, ln_gain, w_in, w_out):
    x, e, w_in, w_out = features[0], delayed_error[0], w_in[0], w_out[0]
    line = lax.axis_size("shard") == 4

    own, own_far = tokens_of(x, e, ln_gain)
    if line:
        first, third = swapped(own, "shard", 1), swapped(own, "shard", 3)
        own_across = across(own_far)
        passing_far, passing_near = passed_on(own, third, after=(own_across,))
        second_far = lax.ppermute(passing_far, "shard", RELAY)
        second_near = lax.ppermute(passing_near, "shard", RELAY)
        first_across = across(far_of(first))
        blocks = [own, first, second_far, third]
        far, second_far = grouped(blocks, False, apart=(2,), after=(first_across,))
        second_across, along = across(second_far), (far_of(third),)
        blocks = [own, first, second_near, third]
        tie = (second_across,)
    else:
        blocks = gathered(own)
        (far,) = grouped(blocks, False)
        far_across = across(far)
        tie, along = (), ()
    far_pair = pair(far)
    prior = forth_and_back((far, far_pair), w_in, w_out)
    near, *pieces = grouped(blocks, True, pieces=PIECES, after=(prior[0],))
    pairs = [pair(piece) for piece in pieces]
    active, pre_error, both = finished(near, pairs, prior, w_out, along, after=tie)
    active_across, pre_error_across = across(active), across(pre_error)
    both_pair = pair(both)
    mine, *others = sums(pre_error, prior[2], w_in)
    count = PIECES if line else 1
    *terms, gain_grad = joined(
        mine, [pair(other) for other in others], far, near, ln_gain, count
    )
    if line:
        own_terms, first_terms, second_terms, third_terms = terms
        second_terms = lax.ppermute(second_terms, "shard", RELAY_BACK)
        first_terms = swapped(first_terms, "shard", 1)
        passing = added(third_terms, second_terms)
        tie = (passing,)
        terms = [own_terms, first_terms, swapped(passing, "shard", 3), second_terms]
        tie = (passing,)
        gain_grad = held(gain_grad, tie)
        active_across = held(active_across, tie)
        far_across = regrouped((own_across, first_across, second_across), active_across)
    else:
        terms = [lax.psum_scatter(terms[0], "shard", scatter_dimension=0, tiled=True)]
    far_across_pair = pair(far_across)
    active_across_pair = pair(active_across)

    tokens = pre_error.shape[0]
    rows = tokens // 2
    piece = pairs[0].shape[0]

    def cut_at(first):
        return [
            (near, first, rows),
            *[(pairs[(first + at) // piece], 0, piece) for at in range(0, rows, piece)],
            (far_across, first, rows),
            (far_across_pair, first, rows),
        ]

    token, w_out_grad = gradient(
        cut_at(rows),
        [(active, 0), (both_pair, 0), (active_across, 0), (active_across_pair, 0)],
        rows, False,
    )
    own_error = own_error_of(x, e, ln_gain, terms, after=(token,))
    n_section = lax.axis_size("section")
    passed = lax.ppermute(
        own_error, "section", [((i + 1) % n_section, i) for i in range(n_section)]
    )
    pre_error_across = held(pre_error_across, (own_error,))
    pre_error_across_pair = pair(pre_error_across)
    gain_grad = held(gain_grad, (own_error, far_across_pair))
    if line:
        gain_grad = total([gain_grad, *[swapped(gain_grad, "shard", mask) for mask in (1, 2, 3)]])
    else:
        gain_grad = summed(gain_grad, "shard")
    gain_parts = [gain_grad, *[swapped(gain_grad, "dp", mask) for mask in (1, 2, 3)]]
    token, w_in_grad = gradient(
        cut_at(0),
        [
            (pre_error, 0), (both_pair, tokens), (pre_error_across, 0),
            (pre_error_across_pair, 0),
        ],
        rows, True, after=(gain_grad,),
    )
    gain_grad = total(gain_parts, after=(token,))
    return passed[None], gain_grad, w_in_grad[None], w_out_grad[None]


def solution(mesh):
    return jax.shard_map(
        per_device,
        mesh=mesh,
        in_specs=(
            P("section", ("dp", "shard"), None),
            P("section", ("dp", "shard"), None),
            P("section", None),
            P("section", None, "shard"),
            P("section", "shard", None),
        ),
        out_specs=(
            P("section", ("dp", "shard"), None),
            P("section", None),
            P("section", "dp", "shard"),
            P("section", "shard", "dp"),
        ),
        check_vma=False,
    )
```

```python
import functools

import jax
import jax.numpy as jnp
from jax import lax
from jax.experimental import pallas as pl
from jax.experimental.pallas import tpu as pltpu
from jax.sharding import PartitionSpec as P

SQRT_HALF = 0.7071067811865476
INV_ROOT_TWO_PI = 0.3989422804014327
EPSILON = 1e-06
MIB = 1024 * 1024
PIECES = 4


def tile_of(extent, largest=512):
    for size in (512, 384, 256, 128):
        if size <= largest and extent % size == 0:
            return size
    return extent


def dot(a, b, a_dim, b_dim):
    return lax.dot_general(
        a, b, (((a_dim,), (b_dim,)), ((), ())), preferred_element_type=jnp.float32
    )


def array(shape, kind):
    return jax.ShapeDtypeStruct(shape, kind)


def window(size, place):
    return pl.ds(pl.multiple_of(place * size, size), size)


def pair_place():
    return lax.axis_index("dp") % 2


def on_end():
    shard = lax.axis_index("shard")
    return (shard == 0) | (shard == lax.axis_size("shard") - 1)


def run(body, arrays, outputs, scratch=(), apart=(), out_apart=(), after=(), limit=None):
    n_in, n_out = len(arrays) + len(apart), len(outputs) + len(out_apart)
    anywhere, near = pl.BlockSpec(memory_space=pl.ANY), pl.BlockSpec(memory_space=pltpu.VMEM)

    def kernel(*refs):
        first = n_in + len(after)
        body(refs[:n_in], refs[first:first + n_out], refs[first + n_out:])

    return pl.pallas_call(
        kernel,
        out_shape=[*outputs, *out_apart],
        in_specs=[near] * len(arrays) + [anywhere] * (len(apart) + len(after)),
        out_specs=[near] * len(outputs) + [anywhere] * len(out_apart),
        scratch_shapes=list(scratch),
        compiler_params=pltpu.CompilerParams(
            vmem_limit_bytes=((limit or 8) if lax.axis_size("shard") == 4 else 58) * MIB
        ),
        cost_estimate=pl.CostEstimate(flops=1000, bytes_accessed=1000, transcendentals=0),
    )(*arrays, *apart, *after)


def normalised(x_ref):
    values = x_ref[...].astype(jnp.float32)
    centred = values - jnp.mean(values, -1, keepdims=True)
    variance = jnp.mean(centred * centred, -1, keepdims=True)
    inverse = lax.rsqrt(variance + EPSILON)
    return centred * inverse, inverse


def far_place():
    return 1 - lax.axis_index("dp") // 2


def near_place():
    return lax.axis_index("dp") // 2


def tokens_of(x, e, gain):
    rows, width = x.shape
    half = width // 2

    def body(ins, outs, scratch):
        x_near, e_near, g_near, sems = scratch
        copies = [
            pltpu.make_async_copy(ins[k], place, sems.at[k])
            for k, place in enumerate((x_near, e_near, g_near))
        ]
        for copy in copies:
            copy.start()
        for copy in copies:
            copy.wait()
        outs[0][:rows, :] = (normalised(x_near)[0] * g_near[...]).astype(x.dtype)
        outs[0][rows:, :] = e_near[...]
        outs[1][...] = outs[0][:, window(half, far_place())]

    return run(
        body, (), [array((2 * rows, width), x.dtype), array((2 * rows, half), x.dtype)],
        apart=(x, e, gain),
        scratch=[
            pltpu.VMEM(x.shape, x.dtype),
            pltpu.VMEM(e.shape, e.dtype),
            pltpu.VMEM(gain.shape, gain.dtype),
            pltpu.SemaphoreType.DMA((3,)),
        ],
        limit=58,
    )


def passed_on(own, came, after=()):
    rows, width = own.shape
    half = width // 2

    def body(ins, outs, scratch):
        for out, place in zip(outs, (far_place(), near_place())):
            columns = window(half, place)
            out[...] = jnp.where(on_end(), ins[0][:, columns], ins[1][:, columns])

    return run(body, (own, came), [array((rows, half), own.dtype)] * 2, after=after)


def far_of(block, after=()):
    rows, width = block.shape
    half = width // 2

    def body(ins, outs, scratch):
        outs[0][...] = ins[0][:, window(half, far_place())]

    return run(body, (block,), [array((rows, half), block.dtype)], after=after)[0]


def grouped(blocks, near, apart=(), pieces=0, after=()):
    half = blocks[0].shape[1] // 2
    rows, kind = blocks[0].shape[0] // 2, blocks[0].dtype
    below = rows * len(blocks)

    def body(ins, outs, scratch):
        columns = window(half, near_place() if near else far_place())
        for k, block in enumerate(ins):
            part = block[...] if block.shape[1] == half else block[:, columns]
            outs[0][k * rows:(k + 1) * rows, :] = part[:rows]
            outs[0][below + k * rows:below + (k + 1) * rows, :] = part[rows:]
            if k in apart:
                at = apart.index(k) * 2 * rows
                outs[1][at:at + 2 * rows, :] = part
        for k in range(pieces):
            at = k * (2 * below // pieces)
            outs[1 + k][...] = outs[0][at:at + 2 * below // pieces, :]

    outs = [array((2 * below, half), kind)]
    if apart:
        outs.append(array((2 * rows * len(apart), half), kind))
    outs += [array((2 * below // pieces, half), kind)] * pieces if pieces else []
    return run(body, blocks, outs, after=after)


def regrouped(blocks, folded, after=()):
    rows, half = blocks[0].shape
    rows //= 2
    count = len(blocks) + 1
    hidden = folded.shape[1]
    first = folded.shape[0] - half // hidden * 2 * rows

    def body(ins, outs, scratch):
        for k, block in enumerate(ins[:-1]):
            outs[0][k * rows:(k + 1) * rows, :] = block[:rows, :]
            outs[0][(count + k) * rows:(count + k + 1) * rows, :] = block[rows:, :]
        for j in range(half // hidden):
            at = first + j * 2 * rows
            columns = slice(j * hidden, (j + 1) * hidden)
            outs[0][(count - 1) * rows:count * rows, columns] = ins[-1][at:at + rows, :]
            outs[0][(2 * count - 1) * rows:, columns] = ins[-1][at + rows:at + 2 * rows, :]

    outs = [array((2 * count * rows, half), blocks[0].dtype)]
    return run(body, (*blocks, folded), outs, after=after)[0]


def held(block, after):
    def body(ins, outs, scratch):
        outs[0][...] = ins[0][...]

    return run(body, (block,), [array(block.shape, block.dtype)], after=after)[0]


def forth_and_back(groups, w_in, w_out, after=()):
    tokens, half = groups[0].shape
    rows, hidden, kind = tokens // 2, w_in.shape[1] // 2, groups[0].dtype
    tile = tile_of(hidden)
    steps = hidden // tile

    def body(ins, outs, scratch):
        w_in_ref, w_out_ref = ins[-2:]
        rows_all, in_weight, out_weight, sems, near_sem = scratch

        def coming(j, forth):
            units = window(tile, pair_place() * steps + j)
            place, depth = window(tile, j), window(half, far_place())
            if forth:
                source, target = w_in_ref.at[depth, units], in_weight.at[:, place]
            else:
                source, target = w_out_ref.at[units, depth], out_weight.at[place, :]
            return pltpu.make_async_copy(source, target, sems.at[1 - int(forth), j])

        along = pltpu.make_async_copy(
            w_in_ref.at[window(half, near_place()), window(hidden, pair_place())],
            outs[2], near_sem,
        )
        for forth in (True, False):
            for j in range(steps):
                coming(j, forth).start()
        along.start()
        for k in range(2):
            rows_all[k * rows:(k + 1) * rows, :] = ins[k][:rows, :]

        @pl.loop(0, steps)
        def _(j):
            coming(j, True).wait()
            place = window(tile, j)
            outs[0][:, place] = dot(rows_all[...], in_weight[:, place], 1, 0)

        for k in range(2):
            rows_all[k * rows:(k + 1) * rows, :] = ins[k][rows:, :]

        @pl.loop(0, steps)
        def _(j):
            coming(j, False).wait()
            place = window(tile, j)
            outs[1][:, place] = dot(rows_all[...], out_weight[place, :], 1, 1)

        along.wait()

    wide = array((tokens, hidden), jnp.float32)
    return run(
        body, groups, [wide, wide, array((half, hidden), kind)], apart=(w_in, w_out),
        scratch=[
            pltpu.VMEM((tokens, half), kind),
            pltpu.VMEM((half, hidden), kind),
            pltpu.VMEM((hidden, half), kind),
            pltpu.SemaphoreType.DMA((2, steps)),
            pltpu.SemaphoreType.DMA,
        ],
        after=after, limit=24,
    )


def finished(group, pairs, prior, w_out, along=(), after=()):
    tokens, half = group.shape
    rows, hidden, kind = tokens // 2, prior[0].shape[1], group.dtype
    tile = tile_of(hidden)
    steps = hidden // tile
    piece = pairs[0].shape[0]
    each = rows // piece

    def body(ins, outs, scratch):
        pre_ref, back_act_ref, in_weight, *more, w_out_ref = ins[1 + 2 * each:]
        rows_all, slope_ref, out_weight, sems = scratch

        def coming(j):
            units = window(tile, pair_place() * steps + j)
            return pltpu.make_async_copy(
                w_out_ref.at[units, window(half, near_place())],
                out_weight.at[window(tile, j), :],
                sems.at[j],
            )

        for j in range(steps):
            coming(j).start()

        def stack(below):
            rows_all[:rows, :] = ins[0][below * rows:(below + 1) * rows, :]
            for k in range(each):
                at = rows + k * piece
                rows_all[at:at + piece, :] = ins[1 + below * each + k][...]

        for block in more:
            for k in range(half // hidden):
                at = tokens + k * block.shape[0]
                outs[0][at:at + block.shape[0], :] = block[:, k * hidden:(k + 1) * hidden]
        stack(0)

        @pl.loop(0, steps)
        def _(j):
            place = window(tile, j)
            pre = pre_ref[:, place] + dot(rows_all[...], in_weight[:, place], 1, 0)
            normal_cdf = 0.5 * (1.0 + lax.erf(pre * SQRT_HALF))
            density = INV_ROOT_TWO_PI * jnp.exp(-0.5 * pre * pre)
            active = (pre * normal_cdf).astype(kind)
            outs[0][:tokens, place] = active
            outs[2][:tokens, place] = active
            slope_ref[:, place] = normal_cdf + pre * density

        stack(1)

        @pl.loop(0, steps)
        def _(j):
            coming(j).wait()
            place = window(tile, j)
            back_act = back_act_ref[:, place] + dot(rows_all[...], out_weight[place, :], 1, 1)
            pre_error = (back_act * slope_ref[:, place]).astype(kind)
            outs[1][:, place] = pre_error
            outs[2][tokens:, place] = pre_error

    below = sum(block.size // hidden for block in along)
    return run(
        body, (group, *pairs, *prior, *along),
        [array((rows, hidden), kind) for rows in (tokens + below, tokens, 2 * tokens)],
        [
            pltpu.VMEM((tokens, half), kind),
            pltpu.VMEM((tokens, hidden), jnp.float32),
            pltpu.VMEM((hidden, half), kind),
            pltpu.SemaphoreType.DMA((steps,)),
        ],
        apart=(w_out,), after=after, limit=18,
    )


def sums(pre_error, near_weight, w_in, after=()):
    tokens, hidden = pre_error.shape
    half, rows, kind = near_weight.shape[0], tokens // 2, pre_error.dtype
    tile = tile_of(half)
    piece = rows // PIECES

    def body(ins, outs, scratch):
        far_weight, sem = scratch
        coming = pltpu.make_async_copy(
            ins[2].at[window(half, far_place()), window(hidden, pair_place())], far_weight, sem
        )
        coming.start()
        for weight, place in ((ins[1], near_place()), (far_weight, far_place())):
            first = place * (half // tile)
            if weight is far_weight:
                coming.wait()

            @pl.loop(0, half // tile)
            def _(j):
                columns = window(tile, first + j)
                term = dot(ins[0][...], weight[window(tile, j), :], 1, 1)
                outs[0][:, columns] = term[:rows]
                for k in range(PIECES):
                    at = rows + k * piece
                    outs[1 + k][:, columns] = term[at:at + piece].astype(kind)

    return run(
        body, (pre_error, near_weight),
        [array((rows, 2 * half), jnp.float32)] + [array((piece, 2 * half), kind)] * PIECES,
        [pltpu.VMEM((half, hidden), kind), pltpu.SemaphoreType.DMA],
        apart=(w_in,), after=after, limit=16,
    )


def joined(mine, others, far, near, gain, count, after=()):
    rows, width = mine.shape
    half = width // 2
    block = rows // count
    kind = others[0].dtype
    piece = rows // PIECES

    def body(ins, outs, scratch):
        mine_ref, others_ref, g_ref = ins[0], ins[1:1 + PIECES], ins[-1]
        for group_ref, place in ((ins[-3], far_place()), (ins[-2], near_place())):
            columns = window(half, place)
            total = jnp.zeros((1, half), jnp.float32)
            for k in range(PIECES):
                here = slice(k * piece, (k + 1) * piece)
                term = mine_ref[here, columns] + others_ref[k][:, columns].astype(jnp.float32)
                term = term.astype(kind)
                if count == PIECES:
                    outs[k][:, columns] = term
                else:
                    outs[0][here, columns] = term
                weighed = term.astype(jnp.float32) * group_ref[here, :].astype(jnp.float32)
                total = total + jnp.sum(weighed, 0, keepdims=True)
            outs[count][:, columns] = total / g_ref[:, columns]

    return run(
        body, (mine, *others, far, near, gain),
        [array((block, width), kind)] * count + [array((1, width), jnp.float32)],
        after=after,
    )


def added(mine, came, after=()):
    def body(ins, outs, scratch):
        came_here = jnp.where(on_end(), 0.0, ins[1][...].astype(jnp.float32))
        outs[0][...] = (ins[0][...].astype(jnp.float32) + came_here).astype(mine.dtype)

    return run(body, (mine, came), [array(mine.shape, mine.dtype)], after=after)[0]


def gradient(cut, full, rows, cut_rows, after=()):
    part, width, kind = full[0][0].shape[1], cut[0][0].shape[1] // 2, full[0][0].dtype
    tile = tile_of(2 * part)
    steps = 2 * part // tile
    shape = (width, 2 * part) if cut_rows else (2 * part, width)

    def body(ins, outs, scratch):
        a_all, b_all, buffer, in_sems, sems = scratch
        lo = pair_place()
        moves, at = [], 0
        for k, (_, first, count) in enumerate(cut):
            source = ins[k].at[pl.ds(first, count), window(width, lo)]
            moves.append((source, a_all.at[pl.ds(at, count), :]))
            at += count
        for k, (_, first) in enumerate(full):
            for half in range(2):
                at = (k // 2 * 2 + (half if k % 2 == 0 else 1 - half)) * rows
                place = window(part, lo if k % 2 == 0 else 1 - lo)
                source = ins[len(cut) + k].at[pl.ds(first + half * rows, rows), :]
                moves.append((source, b_all.at[pl.ds(at, rows), place]))
        copies = [
            pltpu.make_async_copy(a, b, in_sems.at[k]) for k, (a, b) in enumerate(moves)
        ]
        for copy in copies:
            copy.start()
        for copy in copies:
            copy.wait()

        def leaving(j):
            place = window(tile, j)
            target = outs[1].at[:, place] if cut_rows else outs[1].at[place, :]
            return pltpu.make_async_copy(buffer.at[j % 2], target, sems.at[j % 2])

        @pl.loop(0, steps)
        def _(j):
            place = window(tile, j)
            if cut_rows:
                result = dot(a_all[...], b_all[:, place], 0, 0)
            else:
                result = dot(b_all[:, place], a_all[...], 0, 0)

            @pl.when(j >= 2)
            def _():
                leaving(j - 2).wait()

            buffer[j % 2] = result.astype(kind)
            leaving(j).start()

        for j in range(max(steps - 2, 0), steps):
            leaving(j).wait()
        outs[0][...] = jnp.zeros_like(outs[0])

    return run(
        body, (), [array((8, 128), jnp.float32)], out_apart=[array(shape, kind)],
        apart=[a for a, *_ in (*cut, *full)],
        scratch=[
            pltpu.VMEM((4 * rows, width), kind),
            pltpu.VMEM((4 * rows, 2 * part), kind),
            pltpu.VMEM((2, width, tile) if cut_rows else (2, tile, width), kind),
            pltpu.SemaphoreType.DMA((len(cut) + 8,)),
            pltpu.SemaphoreType.DMA((2,)),
        ],
        after=after, limit=16,
    )


def total(parts, after=()):
    def body(ins, outs, scratch):
        sums = [part[...] for part in ins]
        while len(sums) > 1:
            sums = [sums[k] + sums[k + 1] for k in range(0, len(sums), 2)]
        outs[0][...] = sums[0]

    return run(body, parts, [array(parts[0].shape, parts[0].dtype)], after=after)[0]


def own_error_of(x, e, gain, terms, after=()):
    def body(ins, outs, scratch):
        x_ref, e_ref, g_ref = ins[:3]
        total = ins[3][...].astype(jnp.float32)
        for term in ins[4:6]:
            total = total + term[...].astype(jnp.float32)
        for term in ins[6:]:
            total = total + jnp.where(on_end(), term[...].astype(jnp.float32), 0.0)
        scaled = total * g_ref[...]
        centred, inverse = normalised(x_ref)
        corrected = inverse * (
            scaled
            - jnp.mean(scaled, -1, keepdims=True)
            - centred * jnp.mean(scaled * centred, -1, keepdims=True)
        )
        outs[0][...] = (e_ref[...].astype(jnp.float32) + corrected).astype(x.dtype)

    return run(body, (x, e, gain, *terms), [array(x.shape, x.dtype)], after=after)[0]


def swapped(block, axis, mask):
    return lax.ppermute(block, axis, [(i, i ^ mask) for i in range(lax.axis_size(axis))])


def pair(block):
    return swapped(block, "dp", 1)


def across(block):
    return swapped(block, "dp", 2)


def summed(value, axis):
    size = lax.axis_size(axis)
    if size & (size - 1):
        return lax.psum(value, axis)
    mask = 1
    while mask < size:
        value = value + swapped(value, axis, mask)
        mask *= 2
    return value


RELAY = [(0, 2), (3, 1), (2, 3), (1, 0)]
RELAY_BACK = [(b, a) for a, b in RELAY]


def gathered(chunk):
    return [
        lax.all_gather(chunk, "shard", axis=0)[k] for k in range(lax.axis_size("shard"))
    ]


def per_device(features, delayed_error, ln_gain, w_in, w_out):
    x, e, w_in, w_out = features[0], delayed_error[0], w_in[0], w_out[0]
    line = lax.axis_size("shard") == 4

    own, own_far = tokens_of(x, e, ln_gain)
    if line:
        first, third = swapped(own, "shard", 1), swapped(own, "shard", 3)
        own_across = across(own_far)
        own = held(own, (own_across,))
        passing_far, passing_near = passed_on(own, third)
        second_far = lax.ppermute(passing_far, "shard", RELAY)
        second_near = lax.ppermute(passing_near, "shard", RELAY)
        first_across = across(far_of(first))
        blocks = [own, first, second_far, third]
        far, second_far = grouped(blocks, False, apart=(2,), after=(first_across,))
        second_across, along = across(second_far), (far_of(third),)
        blocks = [own, first, second_near, third]
        tie = (second_across,)
    else:
        blocks = gathered(own)
        (far,) = grouped(blocks, False)
        far_across = across(far)
        tie, along = (), ()
    far_pair = pair(far)
    prior = forth_and_back((far, far_pair), w_in, w_out)
    near, *pieces = grouped(blocks, True, pieces=PIECES, after=(prior[0],))
    pairs = [pair(piece) for piece in pieces]
    active, pre_error, both = finished(near, pairs, prior, w_out, along, after=tie)
    active_across, pre_error_across = across(active), across(pre_error)
    both_pair = pair(both)
    mine, *others = sums(pre_error, prior[2], w_in)
    count = PIECES if line else 1
    *terms, gain_grad = joined(
        mine, [pair(other) for other in others], far, near, ln_gain, count
    )
    if line:
        own_terms, first_terms, second_terms, third_terms = terms
        second_terms = lax.ppermute(second_terms, "shard", RELAY_BACK)
        first_terms = swapped(first_terms, "shard", 1)
        passing = added(third_terms, second_terms)
        tie = (passing,)
        terms = [own_terms, first_terms, swapped(passing, "shard", 3), second_terms]
        tie = (passing,)
        gain_grad = held(gain_grad, tie)
        active_across = held(active_across, tie)
        far_across = regrouped((own_across, first_across, second_across), active_across)
    else:
        terms = [lax.psum_scatter(terms[0], "shard", scatter_dimension=0, tiled=True)]
    far_across_pair = pair(far_across)
    active_across_pair = pair(active_across)

    tokens = pre_error.shape[0]
    rows = tokens // 2
    piece = pairs[0].shape[0]

    def cut_at(first):
        return [
            (near, first, rows),
            *[(pairs[(first + at) // piece], 0, piece) for at in range(0, rows, piece)],
            (far_across, first, rows),
            (far_across_pair, first, rows),
        ]

    token, w_out_grad = gradient(
        cut_at(rows),
        [(active, 0), (both_pair, 0), (active_across, 0), (active_across_pair, 0)],
        rows, False,
    )
    gain_grad = held(gain_grad, (token,))
    if line:
        gain_grad = total([gain_grad, *[swapped(gain_grad, "shard", mask) for mask in (1, 2, 3)]])
    else:
        gain_grad = summed(gain_grad, "shard")
    own_error = own_error_of(x, e, ln_gain, terms, after=(gain_grad,))
    n_section = lax.axis_size("section")
    passed = lax.ppermute(
        own_error, "section", [((i + 1) % n_section, i) for i in range(n_section)]
    )
    pre_error_across = held(pre_error_across, (own_error,))
    pre_error_across_pair = pair(pre_error_across)
    gain_grad = held(gain_grad, (own_error,))
    gain_parts = [gain_grad, *[swapped(gain_grad, "dp", mask) for mask in (1, 2, 3)]]
    token, w_in_grad = gradient(
        cut_at(0),
        [
            (pre_error, 0), (both_pair, tokens), (pre_error_across, 0),
            (pre_error_across_pair, 0),
        ],
        rows, True, after=(gain_grad,),
    )
    gain_grad = total(gain_parts, after=(token,))
    passed = held(passed, (token,))
    return passed[None], gain_grad, w_in_grad[None], w_out_grad[None]


def solution(mesh):
    return jax.shard_map(
        per_device,
        mesh=mesh,
        in_specs=(
            P("section", ("dp", "shard"), None),
            P("section", ("dp", "shard"), None),
            P("section", None),
            P("section", None, "shard"),
            P("section", "shard", None),
        ),
        out_specs=(
            P("section", ("dp", "shard"), None),
            P("section", None),
            P("section", "dp", "shard"),
            P("section", "shard", "dp"),
        ),
        check_vma=False,
    )
```
